32 devices in a mesh: head: 2 (over x), seq: 16 (over z, y, core).
Axes of the slice: x: 2, y: 2, z: 4, core: 2. Of those that a mesh axis runs over, the one named last changes fastest.
Arguments:
- queries: bfloat16 [2048, 3072], P(('head', 'seq')), may hold values from -6 to 6
- key_rows: bfloat16 [12288, 3072], P('seq', 'head'), may hold values from -6 to 6
- values: bfloat16 [12288, 3072], P('seq', 'head'), may hold values from -6 to 6
- w_out: bfloat16 [3072, 6144], P('head'), may hold values from -1.1953125 to 1.1953125
- picked: int32 [32, 24], replicated, may hold values from 0 to 191, as said below
- counts: int32 [32], replicated, may hold values from 8 to 24
- tile_home: int32 [192], replicated, may hold values from 0 to 191, as said below
Outputs:
- layer_out: bfloat16 [2048, 6144], P(('head', 'seq'))
The draws below stay inside these ranges and needn't reach their ends.
Inputs may be any that keep to these rules, and one draw needn't show every extreme that they name: `picked`: query tiles j with the same j modulo the number of devices along seq form a group. The used entries of one group are distinct key tiles; key tile t is stored on owner tile_home[t] // 12, and at most 3 used entries of one group are stored on one owner, exactly 3 for some owner in every group. `tile_home`: A permutation of the key tiles.
All inputs are finite; a program needn't handle non-finite values.
Results may differ from the reference program's by a relative error of at most 0.009.
Values may be sent and summed in bfloat16 or wider, within the bound.
A program may use at most 128 MiB of HBM per device.

```python
import jax
import jax.numpy as jnp
from jax import lax

D = 6144
HD = 128
TILE_TOKENS = 64
KT_DEV = 12
MAXSEL = 24
MINSEL = 8
QUERY_FEATURES = 3072
NQT = 32
NQ = 2048
NKT = 192
KEY_TOKENS = 12288
CAP = 3
N_HEAD = 2


def shared_home(key):
    return jax.random.permutation(jax.random.fold_in(key, 11), NKT).astype(jnp.int32)


def draw_tile_home(key, part):
    return shared_home(key)


def draw_picked(key, part):
    home_map = shared_home(key)
    inverse = jnp.zeros((NKT,), jnp.int32).at[home_map].set(jnp.arange(NKT, dtype=jnp.int32))
    seq_count = NKT // KT_DEV
    group_tiles = NQT // seq_count
    slot_count = seq_count * CAP
    base_key = jax.random.fold_in(key, 23)
    hot_owner = jax.random.randint(jax.random.fold_in(base_key, 1), (seq_count,), 0, seq_count).astype(jnp.int32)
    random_part = jax.random.randint(jax.random.fold_in(base_key, 2), (seq_count, slot_count), 0, 1 << 20).astype(jnp.int32)
    slot_ids = jnp.arange(slot_count, dtype=jnp.int32)
    ranking = random_part * slot_count + slot_ids[None, :]
    ranking = ranking + jnp.where(slot_ids[None, :] // CAP == hot_owner[:, None], 1 << 29, 0).astype(jnp.int32)
    slot_order = jnp.argsort(-ranking, axis=1).astype(jnp.int32)[:, :group_tiles * MAXSEL]
    owner_of = slot_order // CAP
    slot_within = slot_order % CAP
    offset = jax.random.randint(jax.random.fold_in(base_key, 3), (seq_count, seq_count), 0, KT_DEV).astype(jnp.int32)
    start_at = jnp.take_along_axis(offset, owner_of, axis=1)
    stored = owner_of * KT_DEV + (start_at + slot_within) % KT_DEV
    chosen = inverse[stored]
    chosen = chosen.reshape(seq_count, MAXSEL, group_tiles).transpose(2, 0, 1).reshape(NQT, MAXSEL)
    return chosen.astype(jnp.int32)


def draw_counts(key, part):
    sampled_tiles = jax.random.randint(jax.random.fold_in(key, 31), (NQT,), MINSEL, MAXSEL + 1).astype(jnp.int32)
    return sampled_tiles.at[0].set(MAXSEL).at[1].set(MINSEL)


def draw_queries(key, part):
    sampled_tiles = jnp.clip(1.5 * jax.random.normal(jax.random.fold_in(key, 5), (NQ, QUERY_FEATURES), jnp.float32), -6.0, 6.0)
    return sampled_tiles.astype(jnp.bfloat16)


def draw_key_rows(key, part):
    sampled_tiles = jnp.clip(jax.random.normal(jax.random.fold_in(key, 7), (KEY_TOKENS, QUERY_FEATURES), jnp.float32), -6.0, 6.0)
    return sampled_tiles.astype(jnp.bfloat16)


def block_scale(rng, extent, split, smallest, largest):
    def one(axis_at, blocks):
        steps = jax.random.uniform(jax.random.fold_in(jax.random.fold_in(rng, 6), axis_at), (blocks,), jnp.float32, smallest / len(split), largest / len(split))
        return jnp.repeat(jnp.exp(steps), extent[axis_at] // blocks).reshape((-1,) + (1,) * (len(extent) - axis_at - 1))

    gain = one(*split[0])
    for cut in split[1:]:
        gain = gain * one(*cut)
    return gain


def gaussian(rng, dims, scale, reach, cuts=(), kind=jnp.bfloat16):
    array = scale * jax.random.normal(rng, dims, jnp.float32)
    if cuts:
        array = array * block_scale(rng, dims, cuts, -0.22, 0.18)
    return jnp.clip(array, -reach, reach).astype(kind)


def setup_inputs(seed: int = 0) -> dict:
    streams_of = jax.random.split(jax.random.key(seed), 8)
    queries = draw_queries(jax.random.fold_in(streams_of[7], 71), 0)
    key_rows = draw_key_rows(jax.random.fold_in(streams_of[7], 71), 0)
    values = gaussian(streams_of[2], (KEY_TOKENS, QUERY_FEATURES), 1.0, 6.0, ((0, 16), (1, 2)))
    w_out = gaussian(streams_of[3], (QUERY_FEATURES, D), 0.2, 1.1953125, ((0, 2),))
    picked = draw_picked(jax.random.fold_in(streams_of[7], 71), 0)
    counts = draw_counts(jax.random.fold_in(streams_of[7], 71), 0)
    tile_home = draw_tile_home(jax.random.fold_in(streams_of[7], 71), 0)
    return {"queries": queries, "key_rows": key_rows, "values": values, "w_out": w_out, "picked": picked, "counts": counts, "tile_home": tile_home}


def reference(queries, key_rows, values, w_out, picked, counts, tile_home):
    width = queries.shape[1]
    head_total = width // HD
    key_tiles = key_rows.reshape(NKT, TILE_TOKENS, width)
    value_tiles = values.reshape(NKT, TILE_TOKENS, width)
    scale = HD ** -0.5

    def attend(tile_index):
        query_tile = lax.dynamic_slice_in_dim(queries, tile_index * TILE_TOKENS, TILE_TOKENS, 0)
        query_tile = query_tile.astype(jnp.float32).reshape(TILE_TOKENS, head_total, HD)
        blocks = tile_home[picked[tile_index]]
        gathered_keys = key_tiles[blocks].astype(jnp.float32).reshape(MAXSEL * TILE_TOKENS, head_total, HD)
        gathered_values = value_tiles[blocks].astype(jnp.float32).reshape(MAXSEL * TILE_TOKENS, head_total, HD)
        logit_scores = jnp.einsum("qhd,khd->hqk", query_tile, gathered_keys) * scale
        is_live = (jnp.arange(MAXSEL * TILE_TOKENS, dtype=jnp.int32) // TILE_TOKENS) < counts[tile_index]
        logit_scores = jnp.where(is_live, logit_scores, -1e30)
        row_top = jnp.max(logit_scores, axis=-1, keepdims=True)
        exponent = jnp.where(is_live, jnp.exp(logit_scores - row_top), 0.0)
        row_sum_total = jnp.sum(exponent, axis=-1)
        weights = lax.optimization_barrier(exponent.astype(jnp.bfloat16)).astype(jnp.float32)
        mixed = jnp.einsum("hqk,khd->qhd", weights, gathered_values) / jnp.transpose(row_sum_total)[:, :, None]
        return mixed.reshape(TILE_TOKENS, width).astype(jnp.bfloat16)

    attended = lax.map(attend, jnp.arange(NQT, dtype=jnp.int32)).reshape(NQ, width)
    group = width // N_HEAD
    result = jnp.zeros((NQ, D), jnp.float32)
    for index in range(N_HEAD):
        part = jnp.dot(attended[:, index * group:(index + 1) * group], w_out[index * group:(index + 1) * group], preferred_element_type=jnp.float32)
        result = result + lax.optimization_barrier(part.astype(jnp.bfloat16)).astype(jnp.float32)
    return result.astype(jnp.bfloat16)
```

```python
import functools

import jax
import jax.numpy as jnp
from jax import lax
from jax.experimental import pallas as pl
from jax.experimental.pallas import tpu as pltpu
from jax.sharding import PartitionSpec as P

HD = 128
NEG = -1e30
MESH = pl.DeviceIdType.MESH
VMEM_BUDGET = 58 * 2**20


def grid_of(seq_count):
    rest = seq_count // 2
    y_size = 1
    for y in range(1, rest + 1):
        if rest % y == 0 and y * y <= rest:
            y_size = y
    return rest // y_size, y_size, 2


def split3(x):
    hi = x.astype(jnp.bfloat16)
    rest = x - hi.astype(jnp.float32)
    mid = rest.astype(jnp.bfloat16)
    low = (rest - mid.astype(jnp.float32)).astype(jnp.bfloat16)
    return hi, mid, low


def pack_stats(rows, lanes):
    stacked = jnp.concatenate(rows, axis=0)
    parts = [p.astype(jnp.float32) for p in split3(stacked)]
    pad = jnp.zeros((16 - 3 * len(rows), lanes), jnp.float32)
    return jnp.concatenate(parts + [pad], axis=0).astype(jnp.bfloat16)


def unpack_stats(block, heads):
    wide = block.astype(jnp.float32)
    return wide[:heads] + wide[heads : 2 * heads] + wide[2 * heads : 3 * heads]


def fused_kernel(cfg, *refs):
    (H, Z, Y, C2, hpc, C, cap, T, NQ, F, attn, proj, DN, N) = cfg
    refs = list(refs)
    take = lambda n: [refs.pop(0) for _ in range(n)]
    if attn:
        q_ref, k_ref, v_ref, off_ref, bias_ref = take(5)
    else:
        (att_ref,) = take(1)
    if proj:
        (w_ref,) = take(1)
    (out_ref,) = take(1)
    if attn:
        qbuf, obuf, r_core, r_y, r_z = take(5)
        (local_sem, xs, xr, zs, zr, ys, yr, cs, cr, rcs, rcr, rys, ryr, rzs, rzr) = take(15)
    if proj:
        wbuf, pbuf, r_x = take(3)
        w_sem, ps, pr = take(3)
        if attn:
            (att_ref,) = take(1)

    head = lax.axis_index("head")
    seq = lax.axis_index("seq")
    core = lax.rem(seq, C2)
    y = lax.rem(lax.div(seq, C2), Y)
    z = lax.div(seq, C2 * Y)

    def seq_of(z_at, y_at, core_at):
        return (z_at * Y + y_at) * C2 + core_at

    def peer_head(i):
        return lax.rem(head + i, H)

    def peer_z(i):
        return lax.rem(z + i, Z)

    def peer_y(i):
        return lax.rem(y + i, Y)

    other = 1 - core
    dev_h = lambda i: {"head": peer_head(i)}
    dev_z = lambda i: {"seq": seq_of(peer_z(i), y, core)}
    dev_y = lambda i: {"seq": seq_of(z, peer_y(i), core)}
    dev_c = {"seq": seq_of(z, y, other)}

    if proj:
        def w_copy(n):
            return pltpu.make_async_copy(
                w_ref.at[:, pl.ds(pl.multiple_of(n * DN, DN), DN)], wbuf.at[n], w_sem.at[n]
            )

    barrier = pltpu.get_barrier_semaphore()
    partners = [dev_h(i) for i in range(1, H)]
    if attn:
        partners += [dev_z(i) for i in range(1, Z)] + [dev_y(i) for i in range(1, Y)] + [dev_c]
    for dev in partners:
        pl.semaphore_signal(barrier, inc=1, device_id=dev, device_id_type=MESH)
    pl.semaphore_wait(barrier, len(partners))

    def remote(src, dst, send, recv, dev):
        return pltpu.make_async_remote_copy(
            src_ref=src, dst_ref=dst, send_sem=send, recv_sem=recv, device_id=dev, device_id_type=MESH
        )

    if attn:
        W = C * F
        rows = pl.ds(pl.multiple_of(head * T, T), T)
        mine = lambda c: qbuf.at[c, core, y, z]

        def feature_cols(h_at, c):
            return pl.ds(pl.multiple_of(h_at * W + c * F, F), F)

        def x_local(c):
            return pltpu.make_async_copy(
                q_ref.at[:, feature_cols(head, c)], mine(c).at[rows, :], local_sem.at[c]
            )

        def x_copy(c, i):
            return remote(
                q_ref.at[:, feature_cols(peer_head(i), c)],
                mine(c).at[rows, :],
                xs.at[c, i],
                xr.at[c, i],
                dev_h(i),
            )

        def z_copy(c, i):
            return remote(mine(c), mine(c), zs.at[c, i], zr.at[c, i], dev_z(i))

        def y_copy(c, i):
            return remote(qbuf.at[c, core, y], qbuf.at[c, core, y], ys.at[c, i], yr.at[c, i], dev_y(i))

        def c_copy(c):
            return remote(qbuf.at[c, core], qbuf.at[c, core], cs.at[c], cr.at[c], dev_c)

        def rc_copy(c):
            return remote(obuf.at[c, other], r_core.at[c], rcs.at[c], rcr.at[c], dev_c)

        def ry_copy(c, i):
            return remote(obuf.at[c, core, peer_y(i)], r_y.at[c, i - 1], rys.at[c, i], ryr.at[c, i], dev_y(i))

        def rz_copy(c, i):
            return remote(obuf.at[c, core, y, peer_z(i)], r_z.at[c, i - 1], rzs.at[c, i], rzr.at[c, i], dev_z(i))

        def merged(blocks, h):
            stats = [s[h : h + 1] for _, s in blocks]
            top = functools.reduce(jnp.maximum, stats)
            weight = [jnp.exp(s - top) for s in stats]
            total = functools.reduce(jnp.add, weight)
            inverse = 1.0 / total
            o = None
            for (block, _), w in zip(blocks, weight):
                part = block[h * HD : (h + 1) * HD, :].astype(jnp.float32) * (w * inverse)
                o = part if o is None else o + part
            return o, top + jnp.log(total)

        def merge_into(dst, sources):
            blocks = [(r, unpack_stats(r[F : F + 16, :], hpc)) for r in [dst] + sources]
            logs = []
            for h in range(hpc):
                o, log = merged(blocks, h)
                dst[h * HD : (h + 1) * HD, :] = o.astype(jnp.bfloat16)
                logs.append(log)
            dst[F : F + 16, :] = pack_stats(logs, NQ)

        scale = HD ** -0.5

        def compute(c):
            @pl.loop(0, C2 * Y * Z)
            def _(g):
                g_core = lax.div(g, Y * Z)
                g_y = lax.rem(lax.div(g, Z), Y)
                g_z = lax.rem(g, Z)
                group = (g_z * Y + g_y) * C2 + g_core
                starts = [off_ref[group * cap + r] for r in range(cap)]
                bias = bias_ref[group]
                logs = []
                for h in range(hpc):
                    cols = slice(c * F + h * HD, c * F + (h + 1) * HD)
                    qh = qbuf[c, g_core, g_y, g_z, :, h * HD : (h + 1) * HD]
                    keys = jnp.concatenate([k_ref[s, :, cols] for s in starts], axis=0)
                    vals = jnp.concatenate([v_ref[s, :, cols] for s in starts], axis=0)
                    scores = lax.dot_general(
                        keys, qh, (((1,), (1,)), ((), ())), preferred_element_type=jnp.float32
                    )
                    scores = jnp.concatenate(
                        [scores[r * T : (r + 1) * T] * scale + bias[r : r + 1] for r in range(cap)], axis=0
                    )
                    top = jnp.max(scores, axis=0, keepdims=True)
                    exponent = jnp.exp(scores - top)
                    total = jnp.sum(exponent, axis=0, keepdims=True)
                    o = lax.dot_general(
                        vals,
                        exponent.astype(jnp.bfloat16),
                        (((0,), (0,)), ((), ())),
                        preferred_element_type=jnp.float32,
                    )
                    obuf[c, g_core, g_y, g_z, h * HD : (h + 1) * HD, :] = (o * (1.0 / total)).astype(jnp.bfloat16)
                    logs.append(top + jnp.log(total))
                obuf[c, g_core, g_y, g_z, F : F + 16, :] = pack_stats(logs, NQ)

        def start_x(c):
            x_local(c).start()
            for i in range(1, H):
                x_copy(c, i).start()

        def step_x(c):
            x_local(c).wait()
            for i in range(1, H):
                rows_in = pl.ds(pl.multiple_of(lax.rem(head - i + H, H) * T, T), T)
                remote(mine(c).at[rows_in, :], mine(c).at[rows_in, :], xs.at[c, i], xr.at[c, i], dev_h(i)).wait_recv()
            for i in range(1, Z):
                z_copy(c, i).start()

        def step_z(c):
            for i in range(1, Z):
                slot = qbuf.at[c, core, y, lax.rem(z - i + Z, Z)]
                remote(slot, slot, zs.at[c, i], zr.at[c, i], dev_z(i)).wait_recv()
            for i in range(1, Y):
                y_copy(c, i).start()

        def step_y(c):
            for i in range(1, Y):
                slot = qbuf.at[c, core, lax.rem(y - i + Y, Y)]
                remote(slot, slot, ys.at[c, i], yr.at[c, i], dev_y(i)).wait_recv()
            c_copy(c).start()

        def step_compute(c):
            slot = qbuf.at[c, other]
            remote(slot, slot, cs.at[c], cr.at[c], dev_c).wait_recv()
            compute(c)
            rc_copy(c).start()

        def step_rc(c):
            rc_copy(c).wait_recv()

            @pl.loop(0, Y * Z)
            def _(g):
                g_y, g_z = lax.div(g, Z), lax.rem(g, Z)
                merge_into(obuf.at[c, core, g_y, g_z], [r_core.at[c, g_y, g_z]])

            for i in range(1, Y):
                ry_copy(c, i).start()

        def step_ry(c):
            for i in range(1, Y):
                ry_copy(c, i).wait_recv()

            @pl.loop(0, Z)
            def _(g_z):
                merge_into(obuf.at[c, core, y, g_z], [r_y.at[c, i, g_z] for i in range(Y - 1)])

            for i in range(1, Z):
                rz_copy(c, i).start()

        att_out = att_ref if proj else out_ref

        def step_rz(c):
            for i in range(1, Z):
                rz_copy(c, i).wait_recv()
            sources = [obuf.at[c, core, y, z]] + [r_z.at[c, i] for i in range(Z - 1)]
            blocks = [(r, unpack_stats(r[F : F + 16, :], hpc)) for r in sources]
            for h in range(hpc):
                o, _ = merged(blocks, h)
                cols = slice(c * F + h * HD, c * F + (h + 1) * HD)
                att_out[:, cols] = jnp.transpose(o).astype(jnp.bfloat16)

        for c in range(C):
            start_x(c)
        if proj:
            @pl.loop(0, N)
            def _(n):
                w_copy(n).start()
        steps = (step_x, step_z, step_y, step_compute, step_rc, step_ry, step_rz)
        for t in range(C + len(steps) - 1):
            for at, step in enumerate(steps):
                if 0 <= t - at < C:
                    step(t - at)
        for c in range(C):
            for i in range(1, H):
                x_copy(c, i).wait_send()
            for i in range(1, Z):
                z_copy(c, i).wait_send()
                rz_copy(c, i).wait_send()
            for i in range(1, Y):
                y_copy(c, i).wait_send()
                ry_copy(c, i).wait_send()
            c_copy(c).wait_send()
            rc_copy(c).wait_send()
    else:
        @pl.loop(0, N)
        def _(n):
            w_copy(n).start()

    if proj:
        def p_copy(n, i):
            return remote(pbuf.at[n, peer_head(i)], r_x.at[n, i - 1], ps.at[n, i], pr.at[n, i], dev_h(i))

        @pl.loop(0, N)
        def _(n):
            w_copy(n).wait()
            part = jnp.dot(att_ref[...], wbuf[n], preferred_element_type=jnp.float32).astype(jnp.bfloat16)
            for h in range(H):
                pbuf[n, h] = part[h * T : (h + 1) * T]
            for i in range(1, H):
                p_copy(n, i).start()

        @pl.loop(0, N)
        def _(n):
            for i in range(1, H):
                p_copy(n, i).wait_recv()
            total = pbuf[n, head].astype(jnp.float32)
            for i in range(H - 1):
                total = total + r_x[n, i].astype(jnp.float32)
            out_ref[:, pl.ds(pl.multiple_of(n * DN, DN), DN)] = total.astype(jnp.bfloat16)
            for i in range(1, H):
                p_copy(n, i).wait_send()


def run_kernel(H, S, T, W, D, cap, kv_rows, attn, proj, operands, cid):
    Z, Y, C2 = grid_of(S)
    NQ = H * T
    heads = W // HD
    hpc = next(n for n in (3, 2, 1) if heads % n == 0)
    C = heads // hpc
    F = hpc * HD
    DN = 512
    N = D // DN
    cfg = (H, Z, Y, C2, hpc, C, cap, T, NQ, F, attn, proj, DN, N)
    bf, dma = jnp.bfloat16, pltpu.SemaphoreType.DMA
    vmem, hbm = pl.BlockSpec(memory_space=pltpu.VMEM), pl.BlockSpec(memory_space=pl.ANY)
    in_specs, scratch = [], []
    if attn:
        in_specs += [vmem, vmem, vmem, pl.BlockSpec(memory_space=pltpu.SMEM), vmem]
        scratch += [
            pltpu.VMEM((C, C2, Y, Z, NQ, F), bf),
            pltpu.VMEM((C, C2, Y, Z, F + 16, NQ), bf),
            pltpu.VMEM((C, Y, Z, F + 16, NQ), bf),
            pltpu.VMEM((C, Y - 1, Z, F + 16, NQ), bf),
            pltpu.VMEM((C, Z - 1, F + 16, NQ), bf),
        ]
        scratch += [dma((C,)), dma((C, H)), dma((C, H)), dma((C, Z)), dma((C, Z)), dma((C, Y)), dma((C, Y))]
        scratch += [dma((C,))] * 4 + [dma((C, Y)), dma((C, Y)), dma((C, Z)), dma((C, Z))]
    else:
        in_specs += [vmem]
    if proj:
        in_specs += [hbm]
        scratch += [
            pltpu.VMEM((N, W, DN), bf),
            pltpu.VMEM((N, H, T, DN), bf),
            pltpu.VMEM((N, H - 1, T, DN), bf),
            dma((N,)),
            dma((N, H)),
            dma((N, H)),
        ]
        if attn:
            scratch += [pltpu.VMEM((NQ, W), bf)]
        out = jax.ShapeDtypeStruct((T, D), bf)
    else:
        out = jax.ShapeDtypeStruct((NQ, W), bf)
    flops = 0
    if attn:
        flops += 4 * S * NQ * cap * T * W
    if proj:
        flops += 2 * NQ * W * D
    return pl.pallas_call(
        functools.partial(fused_kernel, cfg),
        out_shape=out,
        in_specs=in_specs,
        out_specs=vmem,
        scratch_shapes=scratch,
        cost_estimate=pl.CostEstimate(flops=flops, bytes_accessed=2 * (2 * kv_rows * W + W * D), transcendentals=0),
        compiler_params=pltpu.CompilerParams(
            collective_id=cid, has_side_effects=True, vmem_limit_bytes=VMEM_BUDGET
        ),
    )(*operands)


def body(queries, key_rows, values, w_out, picked, counts, tile_home):
    H, S = lax.axis_size("head"), lax.axis_size("seq")
    seq = lax.axis_index("seq")
    T = queries.shape[0]
    W, D = w_out.shape
    kv_rows = key_rows.shape[0]
    tiles_dev = kv_rows // T
    most = picked.shape[1]
    cap = max(2, H * most // S)
    entries = H * most
    tiles = lax.broadcasted_iota(jnp.int32, (1, 1, tile_home.shape[0]), 2)
    stored = jnp.sum(jnp.where(picked[:, :, None] == tiles, tile_home[None, None, :], 0), axis=2)
    live = lax.broadcasted_iota(jnp.int32, picked.shape, 1) < counts[:, None]
    hit = (live & (stored // tiles_dev == seq)).astype(jnp.int32)
    hit = hit.reshape(H, S, most).transpose(1, 0, 2).reshape(S, entries)
    inside = (stored % tiles_dev).reshape(H, S, most).transpose(1, 0, 2).reshape(S, entries)
    at = lax.broadcasted_iota(jnp.int32, (1, entries, entries), 1)
    before = lax.broadcasted_iota(jnp.int32, (1, entries, entries), 2)
    rank = jnp.sum(jnp.where(before < at, hit[:, None, :], 0), axis=2)
    slot = lax.broadcasted_iota(jnp.int32, (1, cap, 1), 1)
    chosen = (hit[:, None, :] > 0) & (rank[:, None, :] == slot)
    offsets = jnp.sum(jnp.where(chosen, inside[:, None, :], 0), axis=2).reshape(S * cap)
    wanted_by = chosen.reshape(S, cap, H, most).any(axis=3)
    bias = jnp.where(jnp.repeat(wanted_by, T, axis=2), 0.0, NEG).astype(jnp.float32)
    bias = jnp.pad(bias, ((0, 0), (0, 8 - cap), (0, 0)))

    key_tiles = key_rows.reshape(tiles_dev, T, W)
    value_tiles = values.reshape(tiles_dev, T, W)
    call = functools.partial(run_kernel, H, S, T)
    whole_bytes = 2 * (2 * S * H * T * W * 2 + 2 * kv_rows * W + W * D)
    if whole_bytes < 52 * 2**20:
        return call(W, D, cap, kv_rows, True, True, (queries, key_tiles, value_tiles, offsets, bias, w_out), 1)
    heads = W // HD
    per = max(n for n in range(1, heads + 1) if heads % n == 0 and 7 * S * H * T * n * HD < 30 * 2**20)
    width = per * HD
    columns = queries.reshape(T, H, W)
    pieces = []
    for p in range(heads // per):
        at = slice(p * width, (p + 1) * width)
        pieces.append(
            call(
                width, D, cap, kv_rows, True, False,
                (columns[:, :, at].reshape(T, H * width), key_tiles[:, :, at], value_tiles[:, :, at], offsets, bias), 1,
            )
        )
    return call(W, D, cap, kv_rows, False, True, (jnp.concatenate(pieces, axis=1), w_out), 2)


def solution(mesh):
    placed = (
        P(("head", "seq"), None),
        P("seq", "head"),
        P("seq", "head"),
        P("head", None),
        P(),
        P(),
        P(),
    )
    return jax.shard_map(
        body, mesh=mesh, in_specs=placed, out_specs=P(("head", "seq"), None), check_vma=False
    )
```

```python
import functools

import jax
import jax.numpy as jnp
from jax import lax
from jax.experimental import pallas as pl
from jax.experimental.pallas import tpu as pltpu
from jax.sharding import PartitionSpec as P

HD = 128
NEG = -1e30
MESH = pl.DeviceIdType.MESH
VMEM_BUDGET = 58 * 2**20


def grid_of(seq_count):
    rest = seq_count // 2
    y_size = 1
    for y in range(1, rest + 1):
        if rest % y == 0 and y * y <= rest:
            y_size = y
    return rest // y_size, y_size, 2


def split3(x):
    hi = x.astype(jnp.bfloat16)
    rest = x - hi.astype(jnp.float32)
    mid = rest.astype(jnp.bfloat16)
    low = (rest - mid.astype(jnp.float32)).astype(jnp.bfloat16)
    return hi, mid, low


def pack_stats(rows, lanes):
    stacked = jnp.concatenate(rows, axis=0)
    parts = [p.astype(jnp.float32) for p in split3(stacked)]
    pad = jnp.zeros((16 - 3 * len(rows), lanes), jnp.float32)
    return jnp.concatenate(parts + [pad], axis=0).astype(jnp.bfloat16)


def unpack_stats(block, heads):
    wide = block.astype(jnp.float32)
    return wide[:heads] + wide[heads : 2 * heads] + wide[2 * heads : 3 * heads]


def fused_kernel(cfg, *refs):
    (H, Z, Y, C2, hpc, C, cap, T, NQ, F, attn, proj, DN, N) = cfg
    refs = list(refs)
    take = lambda n: [refs.pop(0) for _ in range(n)]
    if attn:
        q_ref, k_ref, v_ref, off_ref, bias_ref = take(5)
    else:
        (att_ref,) = take(1)
    if proj:
        (w_ref,) = take(1)
    (out_ref,) = take(1)
    if attn:
        qbuf, obuf, r_core, r_y, r_z = take(5)
        (local_sem, xs, xr, zs, zr, ys, yr, cs, cr, rcs, rcr, rys, ryr, rzs, rzr) = take(15)
    if proj:
        wbuf, pbuf, r_x = take(3)
        w_sem, ps, pr = take(3)
        if attn:
            (att_ref,) = take(1)

    head = lax.axis_index("head")
    seq = lax.axis_index("seq")
    core = lax.rem(seq, C2)
    y = lax.rem(lax.div(seq, C2), Y)
    z = lax.div(seq, C2 * Y)

    def seq_of(z_at, y_at, core_at):
        return (z_at * Y + y_at) * C2 + core_at

    def peer_head(i):
        return lax.rem(head + i, H)

    def peer_z(i):
        return lax.rem(z + i, Z)

    def peer_y(i):
        return lax.rem(y + i, Y)

    other = 1 - core
    dev_h = lambda i: {"head": peer_head(i)}
    dev_z = lambda i: {"seq": seq_of(peer_z(i), y, core)}
    dev_y = lambda i: {"seq": seq_of(z, peer_y(i), core)}
    dev_c = {"seq": seq_of(z, y, other)}

    if proj:
        def w_copy(n):
            return pltpu.make_async_copy(
                w_ref.at[:, pl.ds(pl.multiple_of(n * DN, DN), DN)], wbuf.at[n], w_sem.at[n]
            )

    barrier = pltpu.get_barrier_semaphore()
    partners = [dev_h(i) for i in range(1, H)]
    if attn:
        partners += [dev_z(i) for i in range(1, Z)] + [dev_y(i) for i in range(1, Y)] + [dev_c]
    for dev in partners:
        pl.semaphore_signal(barrier, inc=1, device_id=dev, device_id_type=MESH)
    pl.semaphore_wait(barrier, len(partners))

    def remote(src, dst, send, recv, dev):
        return pltpu.make_async_remote_copy(
            src_ref=src, dst_ref=dst, send_sem=send, recv_sem=recv, device_id=dev, device_id_type=MESH
        )

    if attn:
        W = C * F
        rows = pl.ds(pl.multiple_of(head * T, T), T)
        mine = lambda c: qbuf.at[c, core, y, z]

        def feature_cols(h_at, c):
            return pl.ds(pl.multiple_of(h_at * W + c * F, F), F)

        def x_local(c):
            return pltpu.make_async_copy(
                q_ref.at[:, feature_cols(head, c)], mine(c).at[rows, :], local_sem.at[c]
            )

        def x_copy(c, i):
            return remote(
                q_ref.at[:, feature_cols(peer_head(i), c)],
                mine(c).at[rows, :],
                xs.at[c, i],
                xr.at[c, i],
                dev_h(i),
            )

        def z_copy(c, i):
            return remote(mine(c), mine(c), zs.at[c, i], zr.at[c, i], dev_z(i))

        def y_copy(c, i):
            return remote(qbuf.at[c, core, y], qbuf.at[c, core, y], ys.at[c, i], yr.at[c, i], dev_y(i))

        def c_copy(c):
            return remote(qbuf.at[c, core], qbuf.at[c, core], cs.at[c], cr.at[c], dev_c)

        def rc_copy(c):
            return remote(obuf.at[c, other], r_core.at[c], rcs.at[c], rcr.at[c], dev_c)

        def ry_copy(c, i):
            return remote(obuf.at[c, core, peer_y(i)], r_y.at[c, i - 1], rys.at[c, i], ryr.at[c, i], dev_y(i))

        def rz_copy(c, i):
            return remote(obuf.at[c, core, y, peer_z(i)], r_z.at[c, i - 1], rzs.at[c, i], rzr.at[c, i], dev_z(i))

        def merged(blocks, h):
            stats = [s[h : h + 1] for _, s in blocks]
            top = functools.reduce(jnp.maximum, stats)
            weight = [jnp.exp(s - top) for s in stats]
            total = functools.reduce(jnp.add, weight)
            inverse = 1.0 / total
            o = None
            for (block, _), w in zip(blocks, weight):
                part = block[h * HD : (h + 1) * HD, :].astype(jnp.float32) * (w * inverse)
                o = part if o is None else o + part
            return o, top + jnp.log(total)

        def merge_into(dst, sources):
            blocks = [(r, unpack_stats(r[F : F + 16, :], hpc)) for r in [dst] + sources]
            logs = []
            for h in range(hpc):
                o, log = merged(blocks, h)
                dst[h * HD : (h + 1) * HD, :] = o.astype(jnp.bfloat16)
                logs.append(log)
            dst[F : F + 16, :] = pack_stats(logs, NQ)

        scale = HD ** -0.5

        def compute(c):
            @pl.loop(0, C2 * Y * Z, unroll=2)
            def _(g):
                g_core = lax.div(g, Y * Z)
                g_y = lax.rem(lax.div(g, Z), Y)
                g_z = lax.rem(g, Z)
                group = (g_z * Y + g_y) * C2 + g_core
                starts = [off_ref[group * cap + r] for r in range(cap)]
                bias = bias_ref[group]
                cols = [slice(c * F + h * HD, c * F + (h + 1) * HD) for h in range(hpc)]
                raw = []
                for h in range(hpc):
                    qh = qbuf[c, g_core, g_y, g_z, :, h * HD : (h + 1) * HD]
                    keys = jnp.concatenate([k_ref[s, :, cols[h]] for s in starts], axis=0)
                    raw.append(
                        lax.dot_general(keys, qh, (((1,), (1,)), ((), ())), preferred_element_type=jnp.float32)
                    )
                weights, totals, logs = [], [], []
                for h in range(hpc):
                    scores = jnp.concatenate(
                        [raw[h][r * T : (r + 1) * T] * scale + bias[r : r + 1] for r in range(cap)], axis=0
                    )
                    top = jnp.max(scores, axis=0, keepdims=True)
                    exponent = jnp.exp(scores - top)
                    total = jnp.sum(exponent, axis=0, keepdims=True)
                    weights.append(exponent.astype(jnp.bfloat16))
                    totals.append(total)
                    logs.append(top + jnp.log(total))
                mixed = []
                for h in range(hpc):
                    vals = jnp.concatenate([v_ref[s, :, cols[h]] for s in starts], axis=0)
                    mixed.append(
                        lax.dot_general(
                            vals, weights[h], (((0,), (0,)), ((), ())), preferred_element_type=jnp.float32
                        )
                    )
                for h in range(hpc):
                    obuf[c, g_core, g_y, g_z, h * HD : (h + 1) * HD, :] = (
                        mixed[h] * (1.0 / totals[h])
                    ).astype(jnp.bfloat16)
                obuf[c, g_core, g_y, g_z, F : F + 16, :] = pack_stats(logs, NQ)

        def start_x(c):
            x_local(c).start()
            for i in range(1, H):
                x_copy(c, i).start()

        def step_x(c):
            x_local(c).wait()
            for i in range(1, H):
                rows_in = pl.ds(pl.multiple_of(lax.rem(head - i + H, H) * T, T), T)
                remote(mine(c).at[rows_in, :], mine(c).at[rows_in, :], xs.at[c, i], xr.at[c, i], dev_h(i)).wait_recv()
            for i in range(1, Z):
                z_copy(c, i).start()

        def step_z(c):
            for i in range(1, Z):
                slot = qbuf.at[c, core, y, lax.rem(z - i + Z, Z)]
                remote(slot, slot, zs.at[c, i], zr.at[c, i], dev_z(i)).wait_recv()
            for i in range(1, Y):
                y_copy(c, i).start()

        def step_y(c):
            for i in range(1, Y):
                slot = qbuf.at[c, core, lax.rem(y - i + Y, Y)]
                remote(slot, slot, ys.at[c, i], yr.at[c, i], dev_y(i)).wait_recv()
            c_copy(c).start()

        def step_compute(c):
            slot = qbuf.at[c, other]
            remote(slot, slot, cs.at[c], cr.at[c], dev_c).wait_recv()
            compute(c)
            rc_copy(c).start()

        def step_rc(c):
            rc_copy(c).wait_recv()

            @pl.loop(0, Y * Z)
            def _(g):
                g_y, g_z = lax.div(g, Z), lax.rem(g, Z)
                merge_into(obuf.at[c, core, g_y, g_z], [r_core.at[c, g_y, g_z]])

            for i in range(1, Y):
                ry_copy(c, i).start()

        def step_ry(c):
            for i in range(1, Y):
                ry_copy(c, i).wait_recv()

            @pl.loop(0, Z)
            def _(g_z):
                merge_into(obuf.at[c, core, y, g_z], [r_y.at[c, i, g_z] for i in range(Y - 1)])

            for i in range(1, Z):
                rz_copy(c, i).start()

        att_out = att_ref if proj else out_ref

        def step_rz(c):
            for i in range(1, Z):
                rz_copy(c, i).wait_recv()
            sources = [obuf.at[c, core, y, z]] + [r_z.at[c, i] for i in range(Z - 1)]
            blocks = [(r, unpack_stats(r[F : F + 16, :], hpc)) for r in sources]
            for h in range(hpc):
                o, _ = merged(blocks, h)
                cols = slice(c * F + h * HD, c * F + (h + 1) * HD)
                att_out[:, cols] = jnp.transpose(o).astype(jnp.bfloat16)

        for c in range(C):
            start_x(c)
        if proj:
            @pl.loop(0, N)
            def _(n):
                w_copy(n).start()
        steps = (step_x, step_z, step_y, step_compute, step_rc, step_ry, step_rz)
        for t in range(C + len(steps) - 1):
            for at, step in enumerate(steps):
                if 0 <= t - at < C:
                    step(t - at)
        for c in range(C):
            for i in range(1, H):
                x_copy(c, i).wait_send()
            for i in range(1, Z):
                z_copy(c, i).wait_send()
                rz_copy(c, i).wait_send()
            for i in range(1, Y):
                y_copy(c, i).wait_send()
                ry_copy(c, i).wait_send()
            c_copy(c).wait_send()
            rc_copy(c).wait_send()
    else:
        @pl.loop(0, N)
        def _(n):
            w_copy(n).start()

    if proj:
        def p_copy(n, i):
            return remote(pbuf.at[n, peer_head(i)], r_x.at[n, i - 1], ps.at[n, i], pr.at[n, i], dev_h(i))

        @pl.loop(0, N)
        def _(n):
            w_copy(n).wait()
            part = jnp.dot(att_ref[...], wbuf[n], preferred_element_type=jnp.float32).astype(jnp.bfloat16)
            for h in range(H):
                pbuf[n, h] = part[h * T : (h + 1) * T]
            for i in range(1, H):
                p_copy(n, i).start()

        @pl.loop(0, N)
        def _(n):
            for i in range(1, H):
                p_copy(n, i).wait_recv()
            total = pbuf[n, head].astype(jnp.float32)
            for i in range(H - 1):
                total = total + r_x[n, i].astype(jnp.float32)
            out_ref[:, pl.ds(pl.multiple_of(n * DN, DN), DN)] = total.astype(jnp.bfloat16)
            for i in range(1, H):
                p_copy(n, i).wait_send()


def run_kernel(H, S, T, W, D, cap, kv_rows, attn, proj, operands, cid):
    Z, Y, C2 = grid_of(S)
    NQ = H * T
    heads = W // HD
    hpc = next(n for n in (2, 1) if heads % n == 0)
    C = heads // hpc
    F = hpc * HD
    DN = 512
    N = D // DN
    cfg = (H, Z, Y, C2, hpc, C, cap, T, NQ, F, attn, proj, DN, N)
    bf, dma = jnp.bfloat16, pltpu.SemaphoreType.DMA
    vmem, hbm = pl.BlockSpec(memory_space=pltpu.VMEM), pl.BlockSpec(memory_space=pl.ANY)
    in_specs, scratch = [], []
    if attn:
        in_specs += [vmem, vmem, vmem, pl.BlockSpec(memory_space=pltpu.SMEM), vmem]
        scratch += [
            pltpu.VMEM((C, C2, Y, Z, NQ, F), bf),
            pltpu.VMEM((C, C2, Y, Z, F + 16, NQ), bf),
            pltpu.VMEM((C, Y, Z, F + 16, NQ), bf),
            pltpu.VMEM((C, Y - 1, Z, F + 16, NQ), bf),
            pltpu.VMEM((C, Z - 1, F + 16, NQ), bf),
        ]
        scratch += [dma((C,)), dma((C, H)), dma((C, H)), dma((C, Z)), dma((C, Z)), dma((C, Y)), dma((C, Y))]
        scratch += [dma((C,))] * 4 + [dma((C, Y)), dma((C, Y)), dma((C, Z)), dma((C, Z))]
    else:
        in_specs += [vmem]
    if proj:
        in_specs += [hbm]
        scratch += [
            pltpu.VMEM((N, W, DN), bf),
            pltpu.VMEM((N, H, T, DN), bf),
            pltpu.VMEM((N, H - 1, T, DN), bf),
            dma((N,)),
            dma((N, H)),
            dma((N, H)),
        ]
        if attn:
            scratch += [pltpu.VMEM((NQ, W), bf)]
        out = jax.ShapeDtypeStruct((T, D), bf)
    else:
        out = jax.ShapeDtypeStruct((NQ, W), bf)
    flops = 0
    if attn:
        flops += 4 * S * NQ * cap * T * W
    if proj:
        flops += 2 * NQ * W * D
    return pl.pallas_call(
        functools.partial(fused_kernel, cfg),
        out_shape=out,
        in_specs=in_specs,
        out_specs=vmem,
        scratch_shapes=scratch,
        cost_estimate=pl.CostEstimate(flops=flops, bytes_accessed=2 * (2 * kv_rows * W + W * D), transcendentals=0),
        compiler_params=pltpu.CompilerParams(
            collective_id=cid, has_side_effects=True, vmem_limit_bytes=VMEM_BUDGET
        ),
    )(*operands)


def body(queries, key_rows, values, w_out, picked, counts, tile_home):
    H, S = lax.axis_size("head"), lax.axis_size("seq")
    seq = lax.axis_index("seq")
    T = queries.shape[0]
    W, D = w_out.shape
    kv_rows = key_rows.shape[0]
    tiles_dev = kv_rows // T
    most = picked.shape[1]
    cap = max(2, H * most // S)
    entries = H * most
    tiles = lax.broadcasted_iota(jnp.int32, (1, 1, tile_home.shape[0]), 2)
    stored = jnp.sum(jnp.where(picked[:, :, None] == tiles, tile_home[None, None, :], 0), axis=2)
    live = lax.broadcasted_iota(jnp.int32, picked.shape, 1) < counts[:, None]
    hit = (live & (stored // tiles_dev == seq)).astype(jnp.int32)
    hit = hit.reshape(H, S, most).transpose(1, 0, 2).reshape(S, entries)
    inside = (stored % tiles_dev).reshape(H, S, most).transpose(1, 0, 2).reshape(S, entries)
    at = lax.broadcasted_iota(jnp.int32, (1, entries, entries), 1)
    before = lax.broadcasted_iota(jnp.int32, (1, entries, entries), 2)
    rank = jnp.sum(jnp.where(before < at, hit[:, None, :], 0), axis=2)
    slot = lax.broadcasted_iota(jnp.int32, (1, cap, 1), 1)
    chosen = (hit[:, None, :] > 0) & (rank[:, None, :] == slot)
    offsets = jnp.sum(jnp.where(chosen, inside[:, None, :], 0), axis=2).reshape(S * cap)
    wanted_by = chosen.reshape(S, cap, H, most).any(axis=3)
    bias = jnp.where(jnp.repeat(wanted_by, T, axis=2), 0.0, NEG).astype(jnp.float32)
    bias = jnp.pad(bias, ((0, 0), (0, 8 - cap), (0, 0)))

    key_tiles = key_rows.reshape(tiles_dev, T, W)
    value_tiles = values.reshape(tiles_dev, T, W)
    call = functools.partial(run_kernel, H, S, T)
    whole_bytes = 2 * (2 * S * H * T * W * 2 + 2 * kv_rows * W + W * D)
    if whole_bytes < 52 * 2**20:
        return call(W, D, cap, kv_rows, True, True, (queries, key_tiles, value_tiles, offsets, bias, w_out), 1)
    heads = W // HD
    per = max(n for n in range(1, heads + 1) if heads % n == 0 and 7 * S * H * T * n * HD < 30 * 2**20)
    width = per * HD
    columns = queries.reshape(T, H, W)
    pieces = []
    for p in range(heads // per):
        at = slice(p * width, (p + 1) * width)
        pieces.append(
            call(
                width, D, cap, kv_rows, True, False,
                (columns[:, :, at].reshape(T, H * width), key_tiles[:, :, at], value_tiles[:, :, at], offsets, bias), 1,
            )
        )
    return call(W, D, cap, kv_rows, False, True, (jnp.concatenate(pieces, axis=1), w_out), 2)


def solution(mesh):
    placed = (
        P(("head", "seq"), None),
        P("seq", "head"),
        P("seq", "head"),
        P("head", None),
        P(),
        P(),
        P(),
    )
    return jax.shard_map(
        body, mesh=mesh, in_specs=placed, out_specs=P(("head", "seq"), None), check_vma=False
    )
```

```python
import functools

import jax
import jax.numpy as jnp
from jax import lax
from jax.experimental import pallas as pl
from jax.experimental.pallas import tpu as pltpu
from jax.sharding import PartitionSpec as P

HD = 128
NEG = -1e30
MESH = pl.DeviceIdType.MESH
VMEM_BUDGET = 58 * 2**20


def grid_of(seq_count):
    rest = seq_count // 2
    y_size = 1
    for y in range(1, rest + 1):
        if rest % y == 0 and y * y <= rest:
            y_size = y
    return rest // y_size, y_size, 2


def split3(x):
    hi = x.astype(jnp.bfloat16)
    rest = x - hi.astype(jnp.float32)
    mid = rest.astype(jnp.bfloat16)
    low = (rest - mid.astype(jnp.float32)).astype(jnp.bfloat16)
    return hi, mid, low


def pack_stats(rows, lanes):
    stacked = jnp.concatenate(rows, axis=0)
    parts = [p.astype(jnp.float32) for p in split3(stacked)]
    pad = jnp.zeros((16 - 3 * len(rows), lanes), jnp.float32)
    return jnp.concatenate(parts + [pad], axis=0).astype(jnp.bfloat16)


def unpack_stats(block, heads):
    wide = block.astype(jnp.float32)
    return wide[:heads] + wide[heads : 2 * heads] + wide[2 * heads : 3 * heads]


def fused_kernel(cfg, *refs):
    (H, Z, Y, C2, hpc, C, cap, T, NQ, F, attn, proj, DN, N) = cfg
    refs = list(refs)
    take = lambda n: [refs.pop(0) for _ in range(n)]
    if attn:
        q_ref, k_ref, v_ref, off_ref, bias_ref = take(5)
    else:
        (att_ref,) = take(1)
    if proj:
        (w_ref,) = take(1)
    (out_ref,) = take(1)
    if attn:
        qbuf, obuf, r_core, r_y, r_z = take(5)
        (local_sem, xs, xr, zs, zr, ys, yr, cs, cr, rcs, rcr, rys, ryr, rzs, rzr) = take(15)
    if proj:
        wbuf, pbuf, r_x = take(3)
        w_sem, ps, pr = take(3)
        if attn:
            (att_ref,) = take(1)

    head = lax.axis_index("head")
    seq = lax.axis_index("seq")
    core = lax.rem(seq, C2)
    y = lax.rem(lax.div(seq, C2), Y)
    z = lax.div(seq, C2 * Y)

    def seq_of(z_at, y_at, core_at):
        return (z_at * Y + y_at) * C2 + core_at

    def peer_head(i):
        return lax.rem(head + i, H)

    def peer_z(i):
        return lax.rem(z + i, Z)

    def peer_y(i):
        return lax.rem(y + i, Y)

    other = 1 - core
    dev_h = lambda i: {"head": peer_head(i)}
    dev_z = lambda i: {"seq": seq_of(peer_z(i), y, core)}
    dev_y = lambda i: {"seq": seq_of(z, peer_y(i), core)}
    dev_c = {"seq": seq_of(z, y, other)}

    if proj:
        def w_copy(n):
            return pltpu.make_async_copy(
                w_ref.at[:, pl.ds(pl.multiple_of(n * DN, DN), DN)], wbuf.at[n], w_sem.at[n]
            )

    barrier = pltpu.get_barrier_semaphore()
    partners = [dev_h(i) for i in range(1, H)]
    if attn:
        partners += [dev_z(i) for i in range(1, Z)] + [dev_y(i) for i in range(1, Y)] + [dev_c]
    for dev in partners:
        pl.semaphore_signal(barrier, inc=1, device_id=dev, device_id_type=MESH)
    pl.semaphore_wait(barrier, len(partners))

    def remote(src, dst, send, recv, dev):
        return pltpu.make_async_remote_copy(
            src_ref=src, dst_ref=dst, send_sem=send, recv_sem=recv, device_id=dev, device_id_type=MESH
        )

    if attn:
        W = C * F
        rows = pl.ds(pl.multiple_of(head * T, T), T)
        mine = lambda c: qbuf.at[c, core, y, z]

        def feature_cols(h_at, c):
            return pl.ds(pl.multiple_of(h_at * W + c * F, F), F)

        def x_local(c):
            return pltpu.make_async_copy(
                q_ref.at[:, feature_cols(head, c)], mine(c).at[rows, :], local_sem.at[c]
            )

        def x_copy(c, i):
            return remote(
                q_ref.at[:, feature_cols(peer_head(i), c)],
                mine(c).at[rows, :],
                xs.at[c, i],
                xr.at[c, i],
                dev_h(i),
            )

        def z_copy(c, i):
            return remote(mine(c), mine(c), zs.at[c, i], zr.at[c, i], dev_z(i))

        def y_copy(c, i):
            return remote(qbuf.at[c, core, y], qbuf.at[c, core, y], ys.at[c, i], yr.at[c, i], dev_y(i))

        def c_copy(c):
            return remote(qbuf.at[c, core], qbuf.at[c, core], cs.at[c], cr.at[c], dev_c)

        def rc_copy(c):
            return remote(obuf.at[c, other], r_core.at[c], rcs.at[c], rcr.at[c], dev_c)

        def ry_copy(c, i):
            return remote(obuf.at[c, core, peer_y(i)], r_y.at[c, i - 1], rys.at[c, i], ryr.at[c, i], dev_y(i))

        def rz_copy(c, i):
            return remote(obuf.at[c, core, y, peer_z(i)], r_z.at[c, i - 1], rzs.at[c, i], rzr.at[c, i], dev_z(i))

        def merged(blocks, h):
            stats = [s[h : h + 1] for _, s in blocks]
            top = functools.reduce(jnp.maximum, stats)
            weight = [jnp.exp(s - top) for s in stats]
            total = functools.reduce(jnp.add, weight)
            inverse = 1.0 / total
            o = None
            for (block, _), w in zip(blocks, weight):
                part = block[h * HD : (h + 1) * HD, :].astype(jnp.float32) * (w * inverse)
                o = part if o is None else o + part
            return o, top + jnp.log(total)

        def merge_into(dst, sources):
            blocks = [(r, unpack_stats(r[F : F + 16, :], hpc)) for r in [dst] + sources]
            logs = []
            for h in range(hpc):
                o, log = merged(blocks, h)
                dst[h * HD : (h + 1) * HD, :] = o.astype(jnp.bfloat16)
                logs.append(log)
            dst[F : F + 16, :] = pack_stats(logs, NQ)

        scale = HD ** -0.5

        def compute(c):
            @pl.loop(0, C2 * Y * Z, unroll=4)
            def _(g):
                g_core = lax.div(g, Y * Z)
                g_y = lax.rem(lax.div(g, Z), Y)
                g_z = lax.rem(g, Z)
                group = (g_z * Y + g_y) * C2 + g_core
                starts = [off_ref[group * cap + r] for r in range(cap)]
                bias = bias_ref[group]
                cols = [slice(c * F + h * HD, c * F + (h + 1) * HD) for h in range(hpc)]
                raw = []
                for h in range(hpc):
                    qh = qbuf[c, g_core, g_y, g_z, :, h * HD : (h + 1) * HD]
                    keys = jnp.concatenate([k_ref[s, :, cols[h]] for s in starts], axis=0)
                    raw.append(
                        lax.dot_general(keys, qh, (((1,), (1,)), ((), ())), preferred_element_type=jnp.float32)
                    )
                weights, totals, logs = [], [], []
                for h in range(hpc):
                    scores = jnp.concatenate(
                        [raw[h][r * T : (r + 1) * T] * scale + bias[r : r + 1] for r in range(cap)], axis=0
                    )
                    top = jnp.max(scores, axis=0, keepdims=True)
                    exponent = jnp.exp(scores - top)
                    total = jnp.sum(exponent, axis=0, keepdims=True)
                    weights.append(exponent.astype(jnp.bfloat16))
                    totals.append(total)
                    logs.append(top + jnp.log(total))
                mixed = []
                for h in range(hpc):
                    vals = jnp.concatenate([v_ref[s, :, cols[h]] for s in starts], axis=0)
                    mixed.append(
                        lax.dot_general(
                            vals, weights[h], (((0,), (0,)), ((), ())), preferred_element_type=jnp.float32
                        )
                    )
                for h in range(hpc):
                    obuf[c, g_core, g_y, g_z, h * HD : (h + 1) * HD, :] = (
                        mixed[h] * (1.0 / totals[h])
                    ).astype(jnp.bfloat16)
                obuf[c, g_core, g_y, g_z, F : F + 16, :] = pack_stats(logs, NQ)

        def start_x(c):
            x_local(c).start()
            for i in range(1, H):
                x_copy(c, i).start()

        def step_x(c):
            x_local(c).wait()
            for i in range(1, H):
                rows_in = pl.ds(pl.multiple_of(lax.rem(head - i + H, H) * T, T), T)
                remote(mine(c).at[rows_in, :], mine(c).at[rows_in, :], xs.at[c, i], xr.at[c, i], dev_h(i)).wait_recv()
            for i in range(1, Z):
                z_copy(c, i).start()

        def step_z(c):
            for i in range(1, Z):
                slot = qbuf.at[c, core, y, lax.rem(z - i + Z, Z)]
                remote(slot, slot, zs.at[c, i], zr.at[c, i], dev_z(i)).wait_recv()
            for i in range(1, Y):
                y_copy(c, i).start()

        def step_y(c):
            for i in range(1, Y):
                slot = qbuf.at[c, core, lax.rem(y - i + Y, Y)]
                remote(slot, slot, ys.at[c, i], yr.at[c, i], dev_y(i)).wait_recv()
            c_copy(c).start()

        def step_compute(c):
            slot = qbuf.at[c, other]
            remote(slot, slot, cs.at[c], cr.at[c], dev_c).wait_recv()
            compute(c)
            rc_copy(c).start()

        def step_rc(c):
            rc_copy(c).wait_recv()

            @pl.loop(0, Y * Z)
            def _(g):
                g_y, g_z = lax.div(g, Z), lax.rem(g, Z)
                merge_into(obuf.at[c, core, g_y, g_z], [r_core.at[c, g_y, g_z]])

            for i in range(1, Y):
                ry_copy(c, i).start()

        def step_ry(c):
            for i in range(1, Y):
                ry_copy(c, i).wait_recv()

            @pl.loop(0, Z)
            def _(g_z):
                merge_into(obuf.at[c, core, y, g_z], [r_y.at[c, i, g_z] for i in range(Y - 1)])

            for i in range(1, Z):
                rz_copy(c, i).start()

        att_out = att_ref if proj else out_ref

        def step_rz(c):
            for i in range(1, Z):
                rz_copy(c, i).wait_recv()
            sources = [obuf.at[c, core, y, z]] + [r_z.at[c, i] for i in range(Z - 1)]
            blocks = [(r, unpack_stats(r[F : F + 16, :], hpc)) for r in sources]
            for h in range(hpc):
                o, _ = merged(blocks, h)
                cols = slice(c * F + h * HD, c * F + (h + 1) * HD)
                att_out[:, cols] = jnp.transpose(o).astype(jnp.bfloat16)

        for c in range(C):
            start_x(c)
        if proj:
            @pl.loop(0, N)
            def _(n):
                w_copy(n).start()
        steps = (step_x, step_z, step_y, step_compute, step_rc, step_ry, step_rz)
        for t in range(C + len(steps) - 1):
            for at, step in enumerate(steps):
                if 0 <= t - at < C:
                    step(t - at)
        for c in range(C):
            for i in range(1, H):
                x_copy(c, i).wait_send()
            for i in range(1, Z):
                z_copy(c, i).wait_send()
                rz_copy(c, i).wait_send()
            for i in range(1, Y):
                y_copy(c, i).wait_send()
                ry_copy(c, i).wait_send()
            c_copy(c).wait_send()
            rc_copy(c).wait_send()
    else:
        @pl.loop(0, N)
        def _(n):
            w_copy(n).start()

    if proj:
        def p_copy(n, i):
            return remote(pbuf.at[n, peer_head(i)], r_x.at[n, i - 1], ps.at[n, i], pr.at[n, i], dev_h(i))

        @pl.loop(0, N)
        def _(n):
            w_copy(n).wait()
            part = jnp.dot(att_ref[...], wbuf[n], preferred_element_type=jnp.float32).astype(jnp.bfloat16)
            for h in range(H):
                pbuf[n, h] = part[h * T : (h + 1) * T]
            for i in range(1, H):
                p_copy(n, i).start()

        @pl.loop(0, N)
        def _(n):
            for i in range(1, H):
                p_copy(n, i).wait_recv()
            total = pbuf[n, head].astype(jnp.float32)
            for i in range(H - 1):
                total = total + r_x[n, i].astype(jnp.float32)
            out_ref[:, pl.ds(pl.multiple_of(n * DN, DN), DN)] = total.astype(jnp.bfloat16)
            for i in range(1, H):
                p_copy(n, i).wait_send()


def run_kernel(H, S, T, W, D, cap, kv_rows, attn, proj, operands, cid):
    Z, Y, C2 = grid_of(S)
    NQ = H * T
    heads = W // HD
    hpc = next(n for n in (2, 1) if heads % n == 0)
    C = heads // hpc
    F = hpc * HD
    DN = 512
    N = D // DN
    cfg = (H, Z, Y, C2, hpc, C, cap, T, NQ, F, attn, proj, DN, N)
    bf, dma = jnp.bfloat16, pltpu.SemaphoreType.DMA
    vmem, hbm = pl.BlockSpec(memory_space=pltpu.VMEM), pl.BlockSpec(memory_space=pl.ANY)
    in_specs, scratch = [], []
    if attn:
        in_specs += [vmem, vmem, vmem, pl.BlockSpec(memory_space=pltpu.SMEM), vmem]
        scratch += [
            pltpu.VMEM((C, C2, Y, Z, NQ, F), bf),
            pltpu.VMEM((C, C2, Y, Z, F + 16, NQ), bf),
            pltpu.VMEM((C, Y, Z, F + 16, NQ), bf),
            pltpu.VMEM((C, Y - 1, Z, F + 16, NQ), bf),
            pltpu.VMEM((C, Z - 1, F + 16, NQ), bf),
        ]
        scratch += [dma((C,)), dma((C, H)), dma((C, H)), dma((C, Z)), dma((C, Z)), dma((C, Y)), dma((C, Y))]
        scratch += [dma((C,))] * 4 + [dma((C, Y)), dma((C, Y)), dma((C, Z)), dma((C, Z))]
    else:
        in_specs += [vmem]
    if proj:
        in_specs += [hbm]
        scratch += [
            pltpu.VMEM((N, W, DN), bf),
            pltpu.VMEM((N, H, T, DN), bf),
            pltpu.VMEM((N, H - 1, T, DN), bf),
            dma((N,)),
            dma((N, H)),
            dma((N, H)),
        ]
        if attn:
            scratch += [pltpu.VMEM((NQ, W), bf)]
        out = jax.ShapeDtypeStruct((T, D), bf)
    else:
        out = jax.ShapeDtypeStruct((NQ, W), bf)
    flops = 0
    if attn:
        flops += 4 * S * NQ * cap * T * W
    if proj:
        flops += 2 * NQ * W * D
    return pl.pallas_call(
        functools.partial(fused_kernel, cfg),
        out_shape=out,
        in_specs=in_specs,
        out_specs=vmem,
        scratch_shapes=scratch,
        cost_estimate=pl.CostEstimate(flops=flops, bytes_accessed=2 * (2 * kv_rows * W + W * D), transcendentals=0),
        compiler_params=pltpu.CompilerParams(
            collective_id=cid, has_side_effects=True, vmem_limit_bytes=VMEM_BUDGET
        ),
    )(*operands)


def body(queries, key_rows, values, w_out, picked, counts, tile_home):
    H, S = lax.axis_size("head"), lax.axis_size("seq")
    seq = lax.axis_index("seq")
    T = queries.shape[0]
    W, D = w_out.shape
    kv_rows = key_rows.shape[0]
    tiles_dev = kv_rows // T
    most = picked.shape[1]
    cap = max(2, H * most // S)
    entries = H * most
    tiles = lax.broadcasted_iota(jnp.int32, (1, 1, tile_home.shape[0]), 2)
    stored = jnp.sum(jnp.where(picked[:, :, None] == tiles, tile_home[None, None, :], 0), axis=2)
    live = lax.broadcasted_iota(jnp.int32, picked.shape, 1) < counts[:, None]
    hit = (live & (stored // tiles_dev == seq)).astype(jnp.int32)
    hit = hit.reshape(H, S, most).transpose(1, 0, 2).reshape(S, entries)
    inside = (stored % tiles_dev).reshape(H, S, most).transpose(1, 0, 2).reshape(S, entries)
    at = lax.broadcasted_iota(jnp.int32, (1, entries, entries), 1)
    before = lax.broadcasted_iota(jnp.int32, (1, entries, entries), 2)
    rank = jnp.sum(jnp.where(before < at, hit[:, None, :], 0), axis=2)
    slot = lax.broadcasted_iota(jnp.int32, (1, cap, 1), 1)
    chosen = (hit[:, None, :] > 0) & (rank[:, None, :] == slot)
    offsets = jnp.sum(jnp.where(chosen, inside[:, None, :], 0), axis=2).reshape(S * cap)
    wanted_by = chosen.reshape(S, cap, H, most).any(axis=3)
    bias = jnp.where(jnp.repeat(wanted_by, T, axis=2), 0.0, NEG).astype(jnp.float32)
    bias = jnp.pad(bias, ((0, 0), (0, 8 - cap), (0, 0)))

    key_tiles = key_rows.reshape(tiles_dev, T, W)
    value_tiles = values.reshape(tiles_dev, T, W)
    call = functools.partial(run_kernel, H, S, T)
    whole_bytes = 2 * (2 * S * H * T * W * 2 + 2 * kv_rows * W + W * D)
    if whole_bytes < 52 * 2**20:
        return call(W, D, cap, kv_rows, True, True, (queries, key_tiles, value_tiles, offsets, bias, w_out), 1)
    heads = W // HD
    per = max(n for n in range(1, heads + 1) if heads % n == 0 and 7 * S * H * T * n * HD < 30 * 2**20)
    width = per * HD
    columns = queries.reshape(T, H, W)
    pieces = []
    for p in range(heads // per):
        at = slice(p * width, (p + 1) * width)
        pieces.append(
            call(
                width, D, cap, kv_rows, True, False,
                (columns[:, :, at].reshape(T, H * width), key_tiles[:, :, at], value_tiles[:, :, at], offsets, bias), 1,
            )
        )
    return call(W, D, cap, kv_rows, False, True, (jnp.concatenate(pieces, axis=1), w_out), 2)


def solution(mesh):
    placed = (
        P(("head", "seq"), None),
        P("seq", "head"),
        P("seq", "head"),
        P("head", None),
        P(),
        P(),
        P(),
    )
    return jax.shard_map(
        body, mesh=mesh, in_specs=placed, out_specs=P(("head", "seq"), None), check_vma=False
    )
```
